32 devices in a mesh: group: 2 (over y), replica: 16 (over z, x, core), tensor: 1.
Axes of the slice: x: 2, y: 2, z: 4, core: 2. Of those that a mesh axis runs over, the one named last changes fastest.
Arguments:
- tokens: bfloat16 [32768, 8192], P(('group', 'replica'), 'tensor'), parts along dimension 0, may hold values from -6 to 6
- token_adapter: int32 [32768, 1], P(('group', 'replica')), parts along dimension 0, may hold values from 0 to 31; in each aligned block of 1024 rows (0 to 1023, 1024 to 2047, ...) at most 64 rows name the same one
- adapter_position: int32 [64], P('group'), parts along dimension 0, may hold values from 0 to 31, each once
- replica_live_rows: int32 [32], P(('group', 'replica')), parts along dimension 0, may hold values from 512 to 1024, as said below
- value_weight: bfloat16 [8192, 1024], P('tensor'), may hold values from -0.0625 to 0.0625
- adapter_down_weight: bfloat16 [64, 64, 8192], P(('group', 'replica'), None, 'tensor'), parts along dimension 0, may hold values from -0.0625 to 0.0625
- adapter_up_weight: bfloat16 [64, 64, 1024], P(('group', 'replica'), None, 'tensor'), parts along dimension 0, may hold values from -0.75 to 0.75
Outputs:
- values: bfloat16 [32768, 1024], P(('group', 'replica'), 'tensor'), parts along dimension 0
The draws below stay inside these ranges and needn't reach their ends.
There are 2 independent parts, one for each index of `group`. The reference program is written for one: setup_inputs(seed, part) draws one part's arguments, and reference() takes and returns one part's arrays. A program takes and returns all parts, laid end to end along the dimension named above; an argument that names none is the same for every part. Nothing has to cross between parts.
Inputs may be any that keep to these rules, and one draw needn't show every extreme that they name: `token_adapter`: within each replica's 1024 rows no adapter is named by more than 64 rows, a bound that some block reaches. `replica_live_rows`: some replica has all 1024 rows live.
All inputs are finite; a program needn't handle non-finite values.
Results may differ from the reference program's by a relative error of at most 0.0045.
Values may be sent and summed in bfloat16 or wider, within the bound.
A program may use at most 192 MiB of HBM per device.

```python
import math
import jax
import jax.numpy as jnp
import numpy as np
from jax import lax

MODEL_WIDTH = 8192
VALUE_FEATURES = 1024
ADAPTER_RANK = 64
TOK_DEV = 1024
REPLICAS = 16
ADAPTER_TOTAL = 32
TOKEN_TOTAL = 16384
CAP = 64


def draw_replica_live_rows(key, part):
    key = jax.random.fold_in(key, 7)
    first_key = jax.random.fold_in(key, 1)
    second_key = jax.random.fold_in(key, 2)
    counts = jax.random.randint(first_key, (REPLICAS,), TOK_DEV // 2, TOK_DEV + 1, dtype=jnp.int32)
    chosen = jax.random.randint(second_key, (), 0, REPLICAS, dtype=jnp.int32)
    return jnp.where(jnp.arange(REPLICAS, dtype=jnp.int32) == chosen, TOK_DEV, counts).astype(jnp.int32)


def shard_levels(stream_key, extent, cuts, low, largest):
    loudness, own = 1.0, jax.random.fold_in(stream_key, 6)
    for axis_at, blocks in cuts:
        heights = jnp.exp(jax.random.uniform(jax.random.fold_in(own, axis_at), (blocks,), jnp.float32, low / len(cuts), largest / len(cuts)))
        loudness = loudness * jnp.repeat(heights, extent[axis_at] // blocks).reshape([-1 if axis == axis_at else 1 for axis in range(len(extent))])
    return loudness


def assign_block(stream_key, own, number, rows, count, top, bound, skew):
    sequence = jax.random.permutation(stream_key, count)
    heavy_load, usual = shares(count, rows * top, bound, skew, True), shares(count, rows * top, bound, skew, False)
    places = jnp.arange(count)

    def named(lengths, offset_by):
        used = int((lengths > 0).sum())
        fixed = max(1, used // 4)
        shifted = fixed + (places - fixed + offset_by * (used - fixed)) % max(1, count - fixed)
        return jnp.zeros((count,), jnp.int32).at[sequence[jnp.where(places < fixed, places, shifted)]].set(jnp.asarray(lengths, jnp.int32))

    lengths = jnp.where(number % 4 == 0, named(heavy_load, number // 4), named(usual, number - number // 4 - 1))
    mixed = jax.random.permutation(jax.random.fold_in(own, 3), count)
    source_of, taker = mixed[0:count // 2 * 2:2], mixed[1:count // 2 * 2:2]
    margin = jnp.minimum(lengths[source_of] - 1, bound - lengths[taker]) // 2
    margin = jnp.where((source_of == sequence[0]) | (taker == sequence[0]) | (lengths[taker] == 0), 0, jnp.maximum(margin, 0))
    shifted = jax.random.randint(jax.random.fold_in(own, 4), (count // 2,), 0, 1 << 20) % (margin + 1)
    lengths = lengths.at[source_of].add(-shifted).at[taker].add(shifted)
    labels = jnp.searchsorted(jnp.cumsum(lengths), jnp.arange(rows * top), side="right").astype(jnp.int32)
    grid = labels.reshape(top, rows).T
    grid = grid[jax.random.permutation(jax.random.fold_in(own, 1), rows)]
    offset_by = jax.random.randint(jax.random.fold_in(own, 2), (rows, 1), 0, top)
    return jnp.take_along_axis(grid, (jnp.arange(top)[None, :] + offset_by) % top, axis=1)


def shares(amount, total, limit, skew, full):
    loads = [(1 << 20) // math.isqrt(rank ** skew) + 1 for rank in range(1, amount + 1)]
    largest = limit if full else min(limit, max(-(-total // amount), total * loads[0] // sum(loads)))
    least = 1 if total - largest >= amount - 1 else 0
    holding, rest = [largest] + [least] * (amount - 1), total - largest - least * (amount - 1)
    while rest > 0:
        free = [i for i in range(1, amount) if holding[i] < largest] or [i for i in range(1, amount) if holding[i] < limit]
        whole, remaining = sum([loads[i] for i in free]), rest
        for i in free:
            more = min(limit - holding[i], max(1, remaining * loads[i] // whole), rest)
            holding[i] = holding[i] + more
            rest = rest - more
    return np.array(holding)


def gaussian(own_key, shape, width, most, shards=(), kind=jnp.bfloat16):
    gain = shard_levels(own_key, shape, shards, -0.22, 0.18) if shards else 1.0
    result = jax.random.normal(own_key, shape, jnp.float32) * width * gain
    return jnp.minimum(jnp.maximum(result, -most), most).astype(kind)


def setup_inputs(seed: int = 0, part: int = 0) -> dict:
    keys = jax.random.split(jax.random.key(seed), 8)
    part_keys = jax.random.split(jax.random.fold_in(keys[7], part), 8)
    tokens = gaussian(part_keys[0], (TOKEN_TOTAL, MODEL_WIDTH), 1.0, 6.0, ((0, 16),))
    token_adapter_keys = jax.random.split(jax.random.fold_in(part_keys[1], 1), TOKEN_TOTAL // TOK_DEV)
    token_adapter_turns = jax.random.permutation(jax.random.fold_in(part_keys[1], 3), TOKEN_TOTAL // TOK_DEV)
    token_adapter = jax.vmap(lambda own, number: assign_block(jax.random.fold_in(part_keys[1], 2), own, number, TOK_DEV, ADAPTER_TOTAL, 1, CAP, 2))(token_adapter_keys, token_adapter_turns).reshape((TOKEN_TOTAL, 1))
    adapter_position = jax.random.permutation(part_keys[2], ADAPTER_TOTAL).astype(jnp.int32)
    replica_live_rows = draw_replica_live_rows(jax.random.fold_in(jax.random.fold_in(keys[7], part), 71), part)
    value_weight = gaussian(keys[4], (MODEL_WIDTH, VALUE_FEATURES), MODEL_WIDTH ** -0.5, 0.0625)
    adapter_down_weight = gaussian(part_keys[5], (ADAPTER_TOTAL, ADAPTER_RANK, MODEL_WIDTH), MODEL_WIDTH ** -0.5, 0.0625, ((0, 16),))
    adapter_up_weight = gaussian(part_keys[6], (ADAPTER_TOTAL, ADAPTER_RANK, VALUE_FEATURES), ADAPTER_RANK ** -0.5, 0.75, ((0, 16),))
    return {"tokens": tokens, "token_adapter": token_adapter, "adapter_position": adapter_position, "replica_live_rows": replica_live_rows, "value_weight": value_weight, "adapter_down_weight": adapter_down_weight, "adapter_up_weight": adapter_up_weight}


def reference(tokens, token_adapter, adapter_position, replica_live_rows, value_weight, adapter_down_weight, adapter_up_weight):
    base_output = jnp.dot(tokens, value_weight, preferred_element_type=jnp.float32)
    slot_of = adapter_position[token_adapter[:, 0]].astype(jnp.int32)

    def single_block(block_index):
        first_row = (block_index * 8).astype(jnp.int32)
        rows_per_block = lax.dynamic_slice_in_dim(tokens, first_row, 8, 0).astype(jnp.float32)
        position_select = lax.dynamic_slice_in_dim(slot_of, first_row, 8, 0)
        down_projection_sum = jnp.einsum("fc,fpc->fp", rows_per_block, adapter_down_weight[position_select].astype(jnp.float32))
        reduced_rows = down_projection_sum.astype(jnp.bfloat16).astype(jnp.float32)
        widened_output = jnp.einsum("fl,flh->fh", reduced_rows, adapter_up_weight[position_select].astype(jnp.float32))
        return widened_output.astype(jnp.bfloat16)

    adapter_output = lax.map(single_block, jnp.arange(TOKEN_TOTAL // 8, dtype=jnp.int32)).reshape(TOKEN_TOTAL, VALUE_FEATURES)
    alive_mask = (jnp.arange(TOKEN_TOTAL, dtype=jnp.int32) % TOK_DEV) < jnp.repeat(replica_live_rows, TOK_DEV, total_repeat_length=TOKEN_TOTAL)
    total_output = base_output + adapter_output.astype(jnp.float32)
    return jnp.where(alive_mask[:, None], total_output, 0.0).astype(jnp.bfloat16)
```

```python
import functools

import jax
import jax.numpy as jnp
from jax import lax
from jax.experimental import pallas as pl
from jax.experimental.pallas import tpu as pltpu
from jax.sharding import PartitionSpec as P

MESH = pl.DeviceIdType.MESH
CHUNK_ROWS = 16
BASE_DEPTH = 1024
SHRINK_DEPTH = 1024
TILE = 256


def gather_kernel(
    replicas,
    rank,
    tok_hbm,
    weight_hbm,
    down_hbm,
    up_hbm,
    ident_ref,
    place_ref,
    out_ref,
    every_down,
    every_up,
    tok,
    weight,
    down,
    up,
    slot,
    total,
    shrunk,
    tok_sem,
    weight_sem,
    load_sem,
    ring_send,
    ring_recv,
    pair_send,
    pair_recv,
):
    rows, width = tok.shape
    features = total.shape[1]
    chips = replicas // 2
    half = chips // 2
    chunks = rank // CHUNK_ROWS
    parts = chunks + 1
    base_steps = width // BASE_DEPTH

    me = lax.axis_index("replica")
    core = lax.rem(me, 2)
    chip = me // 2
    column, level = lax.rem(chip, 2), chip // 2
    here = level + column * (chips - 1 - 2 * level)

    def replica_at(place, core_at):
        second = place // half
        level_at = place + second * (chips - 1 - 2 * place)
        return (level_at * 2 + second) * 2 + core_at

    right = replica_at(lax.rem(here + 1, chips), core)
    left = replica_at(lax.rem(here + chips - 1, chips), core)
    sibling = me + 1 - 2 * core

    def owner_slot(step, way, core_at):
        place = lax.rem(here + chips - step + 2 * way * step, chips)
        return replica_at(place, core_at) * 2 + way

    def piece(slot_at, part):
        if part == chunks:
            return every_up.at[slot_at]
        return every_down.at[slot_at, pl.ds(part * CHUNK_ROWS, CHUNK_ROWS)]

    def own_piece(way, part):
        if part == chunks:
            return up_hbm.at[way]
        return down_hbm.at[way, pl.ds(part * CHUNK_ROWS, CHUNK_ROWS)]

    def ring(step, way, part, src):
        at = ((step - 1) * 2 + way) * parts + part
        return pltpu.make_async_remote_copy(
            src_ref=src,
            dst_ref=piece(owner_slot(step - 1, way, core), part),
            send_sem=ring_send.at[at],
            recv_sem=ring_recv.at[at],
            device_id={"replica": left if way else right},
            device_id_type=MESH,
        )

    def ring_arrival(step, way, part):
        at = ((step - 1) * 2 + way) * parts + part
        ref = piece(owner_slot(step, way, core), part)
        return pltpu.make_async_remote_copy(
            src_ref=ref,
            dst_ref=ref,
            send_sem=ring_send.at[at],
            recv_sem=ring_recv.at[at],
            device_id={"replica": right if way else left},
            device_id_type=MESH,
        )

    def pair(step, way, part, src, core_at):
        at = (step * 2 + way) * parts + part
        return pltpu.make_async_remote_copy(
            src_ref=src,
            dst_ref=piece(owner_slot(step, way, core_at), part),
            send_sem=pair_send.at[at],
            recv_sem=pair_recv.at[at],
            device_id={"replica": sibling},
            device_id_type=MESH,
        )

    def tok_load(k):
        cols = pl.ds(pl.multiple_of(k * BASE_DEPTH, BASE_DEPTH), BASE_DEPTH)
        return pltpu.make_async_copy(tok_hbm.at[:, cols], tok.at[:, cols], tok_sem.at[k])

    def weight_load(k):
        depth = pl.ds(pl.multiple_of(k * BASE_DEPTH, BASE_DEPTH), BASE_DEPTH)
        return pltpu.make_async_copy(
            weight_hbm.at[depth], weight.at[lax.rem(k, 2)], weight_sem.at[lax.rem(k, 2)]
        )

    order = [*range(chunks), chunks]

    barrier = pltpu.get_barrier_semaphore()
    for other in (left, right, sibling):
        pl.semaphore_signal(barrier, inc=1, device_id={"replica": other}, device_id_type=MESH)
    pl.semaphore_wait(barrier, 3)

    for part in order:
        for way in range(2):
            ring(1, way, part, own_piece(way, part)).start()
    for part in order:
        for way in range(2):
            pair(0, way, part, own_piece(way, part), core).start()

    weight_load(0).start()
    for k in range(base_steps):
        tok_load(k).start()

    named = ident_ref[...] == lax.broadcasted_iota(jnp.int32, (rows, place_ref.shape[1]), 1)
    slot[...] = jnp.sum(jnp.where(named, place_ref[...], 0), axis=1, keepdims=True)
    total[...] = jnp.zeros_like(total)

    @pl.loop(0, base_steps)
    def _(k):
        @pl.when(k + 1 < base_steps)
        def _():
            weight_load(k + 1).start()

        tok_load(k).wait()
        weight_load(k).wait()
        depth = pl.ds(pl.multiple_of(k * BASE_DEPTH, BASE_DEPTH), BASE_DEPTH)

        @pl.loop(0, features // TILE)
        def _(j):
            cols = pl.ds(pl.multiple_of(j * TILE, TILE), TILE)
            total[:, cols] += jnp.dot(
                tok[:, depth],
                weight[lax.rem(k, 2), :, cols],
                preferred_element_type=jnp.float32,
            )

    def loads(step, own):
        at = lax.rem(step, 2)
        copies = []
        for quarter in range(4):
            way = quarter % 2
            spot = pl.ds(quarter * rank, rank)
            if own and quarter < 2:
                sources = down_hbm.at[way], up_hbm.at[way]
            else:
                whose = core if quarter < 2 else 1 - core
                where = owner_slot(step, way, whose)
                sources = every_down.at[where], every_up.at[where]
            copies.append(
                pltpu.make_async_copy(sources[0], down.at[at, spot], load_sem.at[at, quarter, 0])
            )
            copies.append(
                pltpu.make_async_copy(sources[1], up.at[at, spot], load_sem.at[at, quarter, 1])
            )
        return copies

    def pair_arrivals(step):
        for part in order:
            for way in range(2):
                ref = piece(owner_slot(step, way, 1 - core), part)
                pair(step, way, part, ref, 1 - core).wait_recv()

    def apply(step):
        at = lax.rem(step, 2)
        for copy in loads(step, False):
            copy.wait()
        shrunk[...] = jnp.zeros_like(shrunk)

        @pl.loop(0, width // SHRINK_DEPTH)
        def _(k):
            depth = pl.ds(pl.multiple_of(k * SHRINK_DEPTH, SHRINK_DEPTH), SHRINK_DEPTH)
            shrunk[...] += lax.dot_general(
                tok[:, depth],
                down[at, :, depth],
                (((1,), (1,)), ((), ())),
                preferred_element_type=jnp.float32,
            )

        lane = lax.broadcasted_iota(jnp.int32, (1, 4 * rank), 1)
        lane_slot = owner_slot(step, 1, 1 - core)
        for quarter in (2, 1, 0):
            whose = core if quarter < 2 else 1 - core
            lane_slot = jnp.where(
                lane < (quarter + 1) * rank, owner_slot(step, quarter % 2, whose), lane_slot
            )

        @pl.loop(0, rows // TILE)
        def _(i):
            spot = pl.ds(pl.multiple_of(i * TILE, TILE), TILE)
            chosen = jnp.where(slot[spot] == lane_slot, shrunk[spot], 0.0).astype(jnp.bfloat16)
            delta = jnp.dot(chosen, up[at], preferred_element_type=jnp.float32)
            total[spot] += delta.astype(jnp.bfloat16).astype(jnp.float32)

    pair_arrivals(0)
    for copy in loads(0, True):
        copy.start()

    @pl.loop(1, chips)
    def _(step):
        apply(step - 1)
        for part in order:
            for way in range(2):
                ring_arrival(step, way, part).wait_recv()
                ref = piece(owner_slot(step, way, core), part)

                @pl.when(step + 1 < chips)
                def _():
                    ring(step + 1, way, part, ref).start()

                pair(step, way, part, ref, core).start()
        pair_arrivals(step)
        for copy in loads(step, False):
            copy.start()

    apply(chips - 1)
    out_ref[...] = total[...].astype(jnp.bfloat16)

    for part in order:
        for way in range(2):
            ring(1, way, part, own_piece(way, part)).wait_send()
            pair(0, way, part, own_piece(way, part), core).wait_send()

    @pl.loop(1, chips)
    def _(step):
        for part in order:
            for way in range(2):
                ref = piece(owner_slot(step, way, core), part)

                @pl.when(step + 1 < chips)
                def _():
                    ring(step + 1, way, part, ref).wait_send()

                pair(step, way, part, ref, core).wait_send()


def ring_shards(
    replicas,
    tokens,
    token_adapter,
    adapter_position,
    replica_live_rows,
    value_weight,
    adapter_down_weight,
    adapter_up_weight,
):
    rows, width = tokens.shape
    owned, rank, features = adapter_up_weight.shape
    adapters = adapter_position.shape[0]
    chips = replicas // 2
    parts = rank // CHUNK_ROWS + 1
    any_space = pl.BlockSpec(memory_space=pl.ANY)
    vmem = pl.BlockSpec(memory_space=pltpu.VMEM)
    dma = pltpu.SemaphoreType.DMA
    values, _, _ = pl.pallas_call(
        functools.partial(gather_kernel, replicas, rank),
        out_shape=(
            jax.ShapeDtypeStruct((rows, features), jnp.bfloat16),
            jax.ShapeDtypeStruct((adapters, rank, width), jnp.bfloat16),
            jax.ShapeDtypeStruct((adapters, rank, features), jnp.bfloat16),
        ),
        in_specs=[any_space] * 4 + [vmem] * 2,
        out_specs=(vmem, any_space, any_space),
        scratch_shapes=[
            pltpu.VMEM((rows, width), jnp.bfloat16),
            pltpu.VMEM((2, BASE_DEPTH, features), jnp.bfloat16),
            pltpu.VMEM((2, 4 * rank, width), jnp.bfloat16),
            pltpu.VMEM((2, 4 * rank, features), jnp.bfloat16),
            pltpu.VMEM((rows, 1), jnp.int32),
            pltpu.VMEM((rows, features), jnp.float32),
            pltpu.VMEM((rows, 4 * rank), jnp.float32),
            dma((width // BASE_DEPTH,)),
            dma((2,)),
            dma((2, 4, 2)),
            dma(((chips - 1) * 2 * parts,)),
            dma(((chips - 1) * 2 * parts,)),
            dma((chips * 2 * parts,)),
            dma((chips * 2 * parts,)),
        ],
        compiler_params=pltpu.CompilerParams(
            collective_id=0, has_side_effects=True, vmem_limit_bytes=52 * 2**20
        ),
        cost_estimate=pl.CostEstimate(
            flops=2 * rows * width * (features + adapters * rank)
            + 2 * rows * features * adapters * rank,
            bytes_accessed=2 * (rows * width + width * features + 3 * adapters * rank * width),
            transcendentals=0,
        ),
        name="gather_and_project",
    )(
        tokens,
        value_weight,
        adapter_down_weight,
        adapter_up_weight,
        token_adapter,
        adapter_position[None, :],
    )
    alive = jnp.arange(rows, dtype=jnp.int32) < replica_live_rows[0]
    return jnp.where(alive[:, None], values, jnp.zeros_like(values))


def split_shards(
    tokens,
    token_adapter,
    adapter_position,
    replica_live_rows,
    value_weight,
    adapter_down_weight,
    adapter_up_weight,
):
    rows = tokens.shape[0]
    adapters = adapter_position.shape[0]
    rank = adapter_up_weight.shape[1]
    every_down = lax.all_gather(adapter_down_weight, "replica", axis=0, tiled=True)
    every_up = lax.all_gather(adapter_up_weight, "replica", axis=0, tiled=True)
    base = lax.psum_scatter(
        jnp.dot(tokens, value_weight, preferred_element_type=jnp.float32),
        "tensor",
        scatter_dimension=1,
        tiled=True,
    )
    ids = jnp.arange(adapters, dtype=jnp.int32)[None, :]
    slot = jnp.sum(jnp.where(token_adapter == ids, adapter_position[None, :], 0), axis=1)
    hot = slot[:, None] == ids
    partial = jnp.einsum("td,ard->tar", tokens, every_down, preferred_element_type=jnp.float32)
    partial = jnp.sum(jnp.where(hot[:, :, None], partial, 0.0), axis=1)
    shrunk = lax.psum(partial, "tensor").astype(jnp.bfloat16)
    spread = jnp.where(hot[:, :, None], shrunk[:, None, :], jnp.zeros((), jnp.bfloat16))
    delta = jnp.dot(
        spread.reshape(rows, adapters * rank),
        every_up.reshape(adapters * rank, -1),
        preferred_element_type=jnp.float32,
    ).astype(jnp.bfloat16)
    alive = jnp.arange(rows, dtype=jnp.int32) < replica_live_rows[0]
    return jnp.where(alive[:, None], base + delta.astype(jnp.float32), 0.0).astype(jnp.bfloat16)


def solution(mesh):
    in_specs = (
        P(("group", "replica"), "tensor"),
        P(("group", "replica"), None),
        P("group"),
        P(("group", "replica")),
        P("tensor", None),
        P(("group", "replica"), None, "tensor"),
        P(("group", "replica"), None, "tensor"),
    )
    out_specs = P(("group", "replica"), "tensor")
    if mesh.shape["tensor"] == 1:
        body = functools.partial(ring_shards, mesh.shape["replica"])
    else:
        body = split_shards
    return jax.shard_map(body, mesh=mesh, in_specs=in_specs, out_specs=out_specs, check_vma=False)
```

```python
import functools

import jax
import jax.numpy as jnp
from jax import lax
from jax.experimental import pallas as pl
from jax.experimental.pallas import tpu as pltpu
from jax.sharding import PartitionSpec as P

MESH = pl.DeviceIdType.MESH
CHUNKS = 4
BASE_DEPTH = 1024
TILE = 256


def gather_kernel(
    replicas,
    rank,
    tok_hbm,
    weight_hbm,
    down_hbm,
    up_hbm,
    ident_ref,
    place_ref,
    out_ref,
    every_down,
    every_up,
    tok,
    weight,
    down,
    up,
    slot,
    total,
    shrunk,
    tok_sem,
    weight_sem,
    load_sem,
    ring_send,
    ring_recv,
    pair_send,
    pair_recv,
):
    rows, width = tok.shape
    features = total.shape[1]
    chips = replicas // 2
    half = chips // 2
    chunks = CHUNKS
    parts = chunks + 1
    span = width // chunks
    base_steps = width // BASE_DEPTH
    last = (chips - 1) * chunks - 1

    me = lax.axis_index("replica")
    core = lax.rem(me, 2)
    chip = me // 2
    column, level = lax.rem(chip, 2), chip // 2
    here = level + column * (chips - 1 - 2 * level)

    def replica_at(place, core_at):
        second = place // half
        level_at = place + second * (chips - 1 - 2 * place)
        return (level_at * 2 + second) * 2 + core_at

    right = replica_at(lax.rem(here + 1, chips), core)
    left = replica_at(lax.rem(here + chips - 1, chips), core)
    sibling = me + 1 - 2 * core

    def owner_slot(step, way, core_at):
        place = lax.rem(here + chips - step + 2 * way * step, chips)
        return replica_at(place, core_at) * 2 + way

    def span_of(part):
        return pl.ds(pl.multiple_of(part * span, span), span)

    def piece(slot_at, part):
        if isinstance(part, int) and part == chunks:
            return every_up.at[slot_at]
        return every_down.at[slot_at, :, span_of(part)]

    def own_piece(way, part):
        if isinstance(part, int) and part == chunks:
            return up_hbm.at[way]
        return down_hbm.at[way, :, span_of(part)]

    def ring(step, way, part, src):
        at = ((step - 1) * 2 + way) * parts + part
        return pltpu.make_async_remote_copy(
            src_ref=src,
            dst_ref=piece(owner_slot(step - 1, way, core), part),
            send_sem=ring_send.at[at],
            recv_sem=ring_recv.at[at],
            device_id={"replica": left if way else right},
            device_id_type=MESH,
        )

    def ring_arrival(step, way, part):
        at = ((step - 1) * 2 + way) * parts + part
        ref = piece(owner_slot(step, way, core), part)
        return pltpu.make_async_remote_copy(
            src_ref=ref,
            dst_ref=ref,
            send_sem=ring_send.at[at],
            recv_sem=ring_recv.at[at],
            device_id={"replica": right if way else left},
            device_id_type=MESH,
        )

    def pair(step, way, part, src, core_at):
        at = (step * 2 + way) * parts + part
        return pltpu.make_async_remote_copy(
            src_ref=src,
            dst_ref=piece(owner_slot(step, way, core_at), part),
            send_sem=pair_send.at[at],
            recv_sem=pair_recv.at[at],
            device_id={"replica": sibling},
            device_id_type=MESH,
        )

    def tok_load(k):
        cols = span_of(k)
        return pltpu.make_async_copy(tok_hbm.at[:, cols], tok.at[:, cols], tok_sem.at[k])

    def weight_load(k):
        depth = pl.ds(pl.multiple_of(k * BASE_DEPTH, BASE_DEPTH), BASE_DEPTH)
        return pltpu.make_async_copy(
            weight_hbm.at[depth], weight.at[lax.rem(k, 2)], weight_sem.at[lax.rem(k, 2)]
        )

    order = [chunks, *range(chunks)]

    barrier = pltpu.get_barrier_semaphore()
    for other in (left, right, sibling):
        pl.semaphore_signal(barrier, inc=1, device_id={"replica": other}, device_id_type=MESH)
    pl.semaphore_wait(barrier, 3)

    for part in order:
        for way in range(2):
            ring(1, way, part, own_piece(way, part)).start()
    for part in order:
        for way in range(2):
            pair(0, way, part, own_piece(way, part), core).start()

    for k in range(chunks):
        tok_load(k).start()
    weight_load(0).start()
    weight_load(1).start()

    named = ident_ref[...] == lax.broadcasted_iota(jnp.int32, (rows, place_ref.shape[1]), 1)
    slot[...] = jnp.sum(jnp.where(named, place_ref[...], 0), axis=1, keepdims=True)
    total[...] = jnp.zeros_like(total)

    def base(k):
        weight_load(k).wait()
        depth = pl.ds(pl.multiple_of(k * BASE_DEPTH, BASE_DEPTH), BASE_DEPTH)

        @pl.loop(0, features // TILE)
        def _(j):
            cols = pl.ds(pl.multiple_of(j * TILE, TILE), TILE)
            total[:, cols] += jnp.dot(
                tok[:, depth],
                weight[lax.rem(k, 2), :, cols],
                preferred_element_type=jnp.float32,
            )

        @pl.when(k + 2 < base_steps)
        def _():
            weight_load(k + 2).start()

    def whose(quarter):
        return core if quarter < 2 else 1 - core

    def down_load(step, k, quarter, own=False):
        way = quarter % 2
        src = own_piece(way, k) if own else piece(owner_slot(step, way, whose(quarter)), k)
        return pltpu.make_async_copy(
            src, down.at[pl.ds(quarter * rank, rank)], load_sem.at[quarter, 0]
        )

    def up_load(step, quarter, own=False):
        way = quarter % 2
        src = up_hbm.at[way] if own else every_up.at[owner_slot(step, way, whose(quarter))]
        return pltpu.make_async_copy(
            src, up.at[pl.ds(quarter * rank, rank)], load_sem.at[quarter, 1]
        )

    def arrive(step, part):
        for way in range(2):
            ring_arrival(step, way, part).wait_recv()
            ref = piece(owner_slot(step, way, core), part)

            @pl.when(step + 1 < chips)
            def _():
                ring(step + 1, way, part, ref).start()

            pair(step, way, part, ref, core).start()

    def pair_arrive(step, part):
        for way in range(2):
            ref = piece(owner_slot(step, way, 1 - core), part)
            pair(step, way, part, ref, 1 - core).wait_recv()

    def fetch(step, k, own=False):
        for quarter in range(2):
            down_load(step, k, quarter, own).start()

        @pl.when(k == 0)
        def _():
            for quarter in range(2):
                up_load(step, quarter, own).start()
            pair_arrive(step, chunks)
            for quarter in range(2, 4):
                up_load(step, quarter).start()

        pair_arrive(step, k)
        for quarter in range(2, 4):
            down_load(step, k, quarter).start()

    def shrink(step, k):
        for quarter in range(4):
            down_load(step, k, quarter).wait()

        def product():
            return lax.dot_general(
                tok[:, span_of(k)],
                down[...],
                (((1,), (1,)), ((), ())),
                preferred_element_type=jnp.float32,
            )

        @pl.when(k == 0)
        def _():
            shrunk[...] = jnp.zeros_like(shrunk)

        shrunk[...] += product()

    def widen(step, store):
        for quarter in range(4):
            up_load(step, quarter).wait()
        lane = lax.broadcasted_iota(jnp.int32, (1, 4 * rank), 1)
        lane_slot = owner_slot(step, 1, 1 - core)
        for quarter in (2, 1, 0):
            lane_slot = jnp.where(
                lane < (quarter + 1) * rank,
                owner_slot(step, quarter % 2, whose(quarter)),
                lane_slot,
            )

        @pl.loop(0, rows // TILE)
        def _(i):
            spot = pl.ds(pl.multiple_of(i * TILE, TILE), TILE)
            chosen = jnp.where(slot[spot] == lane_slot, shrunk[spot], 0.0).astype(jnp.bfloat16)
            delta = jnp.dot(chosen, up[...], preferred_element_type=jnp.float32)
            result = total[spot] + delta.astype(jnp.bfloat16).astype(jnp.float32)
            if store:
                out_ref[spot] = result.astype(jnp.bfloat16)
            else:
                total[spot] = result

    def apply(step, k):
        shrink(step, k)

        @pl.when(k == chunks - 1)
        def _():
            widen(step, False)

    @pl.loop(0, chunks)
    def _(k):
        tok_load(k).wait()
        fetch(0, k, True)
        apply(0, k)

    @pl.loop(0, last + 1)
    def _(unit):
        step, k = unit // chunks + 1, lax.rem(unit, chunks)
        before, before_k = (unit - 1) // chunks + 1, lax.rem(unit + chunks - 1, chunks)

        @pl.when(unit == last)
        def _():
            apply(before, before_k)

        @pl.when(k == 0)
        def _():
            arrive(step, chunks)

        arrive(step, k)

        @pl.when(unit * (last - unit) > 0)
        def _():
            apply(before, before_k)

        fetch(step, k)

        @pl.when(unit < base_steps)
        def _():
            base(unit)

    shrink(chips - 1, chunks - 1)
    widen(chips - 1, True)

    for part in order:
        for way in range(2):
            ring(1, way, part, own_piece(way, part)).wait_send()
            pair(0, way, part, own_piece(way, part), core).wait_send()

    @pl.loop(1, chips)
    def _(step):
        for part in order:
            for way in range(2):
                ref = piece(owner_slot(step, way, core), part)

                @pl.when(step + 1 < chips)
                def _():
                    ring(step + 1, way, part, ref).wait_send()

                pair(step, way, part, ref, core).wait_send()


def ring_shards(
    replicas,
    tokens,
    token_adapter,
    adapter_position,
    replica_live_rows,
    value_weight,
    adapter_down_weight,
    adapter_up_weight,
):
    rows, width = tokens.shape
    owned, rank, features = adapter_up_weight.shape
    adapters = adapter_position.shape[0]
    chips = replicas // 2
    parts = CHUNKS + 1
    any_space = pl.BlockSpec(memory_space=pl.ANY)
    vmem = pl.BlockSpec(memory_space=pltpu.VMEM)
    dma = pltpu.SemaphoreType.DMA
    values, _, _ = pl.pallas_call(
        functools.partial(gather_kernel, replicas, rank),
        out_shape=(
            jax.ShapeDtypeStruct((rows, features), jnp.bfloat16),
            jax.ShapeDtypeStruct((adapters, rank, width), jnp.bfloat16),
            jax.ShapeDtypeStruct((adapters, rank, features), jnp.bfloat16),
        ),
        in_specs=[any_space] * 4 + [vmem] * 2,
        out_specs=(vmem, any_space, any_space),
        scratch_shapes=[
            pltpu.VMEM((rows, width), jnp.bfloat16),
            pltpu.VMEM((2, BASE_DEPTH, features), jnp.bfloat16),
            pltpu.VMEM((4 * rank, width // CHUNKS), jnp.bfloat16),
            pltpu.VMEM((4 * rank, features), jnp.bfloat16),
            pltpu.VMEM((rows, 1), jnp.int32),
            pltpu.VMEM((rows, features), jnp.float32),
            pltpu.VMEM((rows, 4 * rank), jnp.float32),
            dma((CHUNKS,)),
            dma((2,)),
            dma((4, 2)),
            dma(((chips - 1) * 2 * parts,)),
            dma(((chips - 1) * 2 * parts,)),
            dma((chips * 2 * parts,)),
            dma((chips * 2 * parts,)),
        ],
        compiler_params=pltpu.CompilerParams(
            collective_id=0, has_side_effects=True, vmem_limit_bytes=52 * 2**20
        ),
        cost_estimate=pl.CostEstimate(
            flops=2 * rows * width * (features + adapters * rank)
            + 2 * rows * features * adapters * rank,
            bytes_accessed=2 * (rows * width + width * features + 3 * adapters * rank * width),
            transcendentals=0,
        ),
        name="gather_and_project",
    )(
        tokens,
        value_weight,
        adapter_down_weight,
        adapter_up_weight,
        token_adapter,
        adapter_position[None, :],
    )
    alive = jnp.arange(rows, dtype=jnp.int32) < replica_live_rows[0]
    return jnp.where(alive[:, None], values, jnp.zeros_like(values))


def split_shards(
    tokens,
    token_adapter,
    adapter_position,
    replica_live_rows,
    value_weight,
    adapter_down_weight,
    adapter_up_weight,
):
    rows = tokens.shape[0]
    adapters = adapter_position.shape[0]
    rank = adapter_up_weight.shape[1]
    every_down = lax.all_gather(adapter_down_weight, "replica", axis=0, tiled=True)
    every_up = lax.all_gather(adapter_up_weight, "replica", axis=0, tiled=True)
    base = lax.psum_scatter(
        jnp.dot(tokens, value_weight, preferred_element_type=jnp.float32),
        "tensor",
        scatter_dimension=1,
        tiled=True,
    )
    ids = jnp.arange(adapters, dtype=jnp.int32)[None, :]
    slot = jnp.sum(jnp.where(token_adapter == ids, adapter_position[None, :], 0), axis=1)
    hot = slot[:, None] == ids
    partial = jnp.einsum("td,ard->tar", tokens, every_down, preferred_element_type=jnp.float32)
    partial = jnp.sum(jnp.where(hot[:, :, None], partial, 0.0), axis=1)
    shrunk = lax.psum(partial, "tensor").astype(jnp.bfloat16)
    spread = jnp.where(hot[:, :, None], shrunk[:, None, :], jnp.zeros((), jnp.bfloat16))
    delta = jnp.dot(
        spread.reshape(rows, adapters * rank),
        every_up.reshape(adapters * rank, -1),
        preferred_element_type=jnp.float32,
    ).astype(jnp.bfloat16)
    alive = jnp.arange(rows, dtype=jnp.int32) < replica_live_rows[0]
    return jnp.where(alive[:, None], base + delta.astype(jnp.float32), 0.0).astype(jnp.bfloat16)


def solution(mesh):
    in_specs = (
        P(("group", "replica"), "tensor"),
        P(("group", "replica"), None),
        P("group"),
        P(("group", "replica")),
        P("tensor", None),
        P(("group", "replica"), None, "tensor"),
        P(("group", "replica"), None, "tensor"),
    )
    out_specs = P(("group", "replica"), "tensor")
    if mesh.shape["tensor"] == 1:
        body = functools.partial(ring_shards, mesh.shape["replica"])
    else:
        body = split_shards
    return jax.shard_map(body, mesh=mesh, in_specs=in_specs, out_specs=out_specs, check_vma=False)
```

```python
import functools

import jax
import jax.numpy as jnp
from jax import lax
from jax.experimental import pallas as pl
from jax.experimental.pallas import tpu as pltpu
from jax.sharding import PartitionSpec as P

MESH = pl.DeviceIdType.MESH
CHUNKS = 4
BASE_DEPTH = 1024
TILE = 256
LANES = 128


def gather_kernel(
    replicas,
    rank,
    tok_hbm,
    weight_hbm,
    down_hbm,
    up_hbm,
    slot_ref,
    out_ref,
    every_down,
    every_up,
    tok,
    weight,
    down,
    up,
    slot,
    total,
    shrunk,
    tok_sem,
    weight_sem,
    load_sem,
    ring_send,
    ring_recv,
    pair_send,
    pair_recv,
):
    rows, width = tok.shape
    features = total.shape[1]
    chips = replicas // 2
    half = chips // 2
    chunks = CHUNKS
    parts = chunks + 1
    span = width // chunks
    base_steps = width // BASE_DEPTH
    last = (chips - 1) * chunks - 1

    me = lax.axis_index("replica")
    core = lax.rem(me, 2)
    chip = me // 2
    column, level = lax.rem(chip, 2), chip // 2
    here = level + column * (chips - 1 - 2 * level)

    def replica_at(place, core_at):
        second = place // half
        level_at = place + second * (chips - 1 - 2 * place)
        return (level_at * 2 + second) * 2 + core_at

    right = replica_at(lax.rem(here + 1, chips), core)
    left = replica_at(lax.rem(here + chips - 1, chips), core)
    sibling = me + 1 - 2 * core

    def owner_slot(step, way, core_at):
        place = lax.rem(here + chips - step + 2 * way * step, chips)
        return replica_at(place, core_at) * 2 + way

    def span_of(part):
        return pl.ds(pl.multiple_of(part * span, span), span)

    def piece(slot_at, part):
        if isinstance(part, int) and part == chunks:
            return every_up.at[slot_at]
        return every_down.at[slot_at, :, span_of(part)]

    def own_piece(way, part):
        if isinstance(part, int) and part == chunks:
            return up_hbm.at[way]
        return down_hbm.at[way, :, span_of(part)]

    def ring(step, way, part, src):
        at = ((step - 1) * 2 + way) * parts + part
        return pltpu.make_async_remote_copy(
            src_ref=src,
            dst_ref=piece(owner_slot(step - 1, way, core), part),
            send_sem=ring_send.at[at],
            recv_sem=ring_recv.at[at],
            device_id={"replica": left if way else right},
            device_id_type=MESH,
        )

    def ring_arrival(step, way, part):
        at = ((step - 1) * 2 + way) * parts + part
        ref = piece(owner_slot(step, way, core), part)
        return pltpu.make_async_remote_copy(
            src_ref=ref,
            dst_ref=ref,
            send_sem=ring_send.at[at],
            recv_sem=ring_recv.at[at],
            device_id={"replica": right if way else left},
            device_id_type=MESH,
        )

    def pair(step, way, part, src, core_at):
        at = (step * 2 + way) * parts + part
        return pltpu.make_async_remote_copy(
            src_ref=src,
            dst_ref=piece(owner_slot(step, way, core_at), part),
            send_sem=pair_send.at[at],
            recv_sem=pair_recv.at[at],
            device_id={"replica": sibling},
            device_id_type=MESH,
        )

    def tok_load(k):
        cols = span_of(k)
        return pltpu.make_async_copy(tok_hbm.at[:, cols], tok.at[:, cols], tok_sem.at[k])

    def weight_load(k):
        depth = pl.ds(pl.multiple_of(k * BASE_DEPTH, BASE_DEPTH), BASE_DEPTH)
        return pltpu.make_async_copy(
            weight_hbm.at[depth], weight.at[lax.rem(k, 2)], weight_sem.at[lax.rem(k, 2)]
        )

    order = [chunks, *range(chunks)]

    barrier = pltpu.get_barrier_semaphore()
    for other in (left, right, sibling):
        pl.semaphore_signal(barrier, inc=1, device_id={"replica": other}, device_id_type=MESH)
    pl.semaphore_wait(barrier, 3)

    for part in order:
        for way in range(2):
            ring(1, way, part, own_piece(way, part)).start()
    for part in order:
        for way in range(2):
            pair(0, way, part, own_piece(way, part), core).start()

    for k in range(chunks):
        tok_load(k).start()
    weight_load(0).start()
    weight_load(1).start()

    diagonal = lax.broadcasted_iota(jnp.int32, (LANES, LANES), 0) == lax.broadcasted_iota(
        jnp.int32, (LANES, LANES), 1
    )
    for block in range(rows // LANES):
        row = slot_ref[block : block + 1, :]
        slot[pl.ds(block * LANES, LANES)] = jnp.sum(
            jnp.where(diagonal, row, 0), axis=1, keepdims=True
        )
    total[...] = jnp.zeros_like(total)

    def base(k):
        weight_load(k).wait()
        depth = pl.ds(pl.multiple_of(k * BASE_DEPTH, BASE_DEPTH), BASE_DEPTH)

        @pl.loop(0, features // TILE)
        def _(j):
            cols = pl.ds(pl.multiple_of(j * TILE, TILE), TILE)
            total[:, cols] += jnp.dot(
                tok[:, depth],
                weight[lax.rem(k, 2), :, cols],
                preferred_element_type=jnp.float32,
            )

        @pl.when(k + 2 < base_steps)
        def _():
            weight_load(k + 2).start()

    def whose(quarter):
        return core if quarter < 2 else 1 - core

    def down_load(step, k, quarter, own=False):
        way = quarter % 2
        src = own_piece(way, k) if own else piece(owner_slot(step, way, whose(quarter)), k)
        return pltpu.make_async_copy(
            src, down.at[pl.ds(quarter * rank, rank)], load_sem.at[quarter, 0]
        )

    def up_load(step, quarter, own=False):
        way = quarter % 2
        src = up_hbm.at[way] if own else every_up.at[owner_slot(step, way, whose(quarter))]
        return pltpu.make_async_copy(
            src, up.at[pl.ds(quarter * rank, rank)], load_sem.at[quarter, 1]
        )

    def arrive(step, part):
        for way in range(2):
            ring_arrival(step, way, part).wait_recv()
            ref = piece(owner_slot(step, way, core), part)

            @pl.when(step + 1 < chips)
            def _():
                ring(step + 1, way, part, ref).start()

            pair(step, way, part, ref, core).start()

    def pair_arrive(step, part):
        for way in range(2):
            ref = piece(owner_slot(step, way, 1 - core), part)
            pair(step, way, part, ref, 1 - core).wait_recv()

    def fetch(step, k, own=False):
        for quarter in range(2):
            down_load(step, k, quarter, own).start()

        @pl.when(k == 0)
        def _():
            for quarter in range(2):
                up_load(step, quarter, own).start()
            pair_arrive(step, chunks)
            for quarter in range(2, 4):
                up_load(step, quarter).start()

        pair_arrive(step, k)
        for quarter in range(2, 4):
            down_load(step, k, quarter).start()

    def shrink(step, k):
        for quarter in range(4):
            down_load(step, k, quarter).wait()

        def product():
            return lax.dot_general(
                tok[:, span_of(k)],
                down[...],
                (((1,), (1,)), ((), ())),
                preferred_element_type=jnp.float32,
            )

        @pl.when(k == 0)
        def _():
            shrunk[...] = jnp.zeros_like(shrunk)

        shrunk[...] += product()

    def widen(step, store):
        for quarter in range(4):
            up_load(step, quarter).wait()
        lane = lax.broadcasted_iota(jnp.int32, (1, 4 * rank), 1)
        lane_slot = owner_slot(step, 1, 1 - core)
        for quarter in (2, 1, 0):
            lane_slot = jnp.where(
                lane < (quarter + 1) * rank,
                owner_slot(step, quarter % 2, whose(quarter)),
                lane_slot,
            )

        @pl.loop(0, rows // TILE)
        def _(i):
            spot = pl.ds(pl.multiple_of(i * TILE, TILE), TILE)
            chosen = jnp.where(slot[spot] == lane_slot, shrunk[spot], 0.0).astype(jnp.bfloat16)
            delta = jnp.dot(chosen, up[...], preferred_element_type=jnp.float32)
            result = total[spot] + delta.astype(jnp.bfloat16).astype(jnp.float32)
            if store:
                out_ref[spot] = result.astype(jnp.bfloat16)
            else:
                total[spot] = result

    def apply(step, k):
        shrink(step, k)

        @pl.when(k == chunks - 1)
        def _():
            widen(step, False)

    def sent(first, end):
        @pl.loop(first, end)
        def _(step):
            for part in order:
                for way in range(2):
                    ref = piece(owner_slot(step, way, core), part)

                    @pl.when(step + 1 < chips)
                    def _():
                        ring(step + 1, way, part, ref).wait_send()

                    pair(step, way, part, ref, core).wait_send()

    @pl.loop(0, chunks)
    def _(k):
        tok_load(k).wait()
        fetch(0, k, True)
        apply(0, k)

    @pl.loop(0, last + 1)
    def _(unit):
        step, k = unit // chunks + 1, lax.rem(unit, chunks)
        before, before_k = (unit - 1) // chunks + 1, lax.rem(unit + chunks - 1, chunks)

        @pl.when(unit == last)
        def _():
            apply(before, before_k)
            for part in order:
                for way in range(2):
                    ring(1, way, part, own_piece(way, part)).wait_send()
                    pair(0, way, part, own_piece(way, part), core).wait_send()
            sent(1, chips - 2)

        @pl.when(k == 0)
        def _():
            arrive(step, chunks)

        arrive(step, k)

        @pl.when(unit * (last - unit) > 0)
        def _():
            apply(before, before_k)

        fetch(step, k)

        @pl.when(unit < base_steps)
        def _():
            base(unit)

    shrink(chips - 1, chunks - 1)
    widen(chips - 1, True)

    sent(chips - 2, chips)


def ring_shards(
    replicas,
    tokens,
    token_adapter,
    adapter_position,
    replica_live_rows,
    value_weight,
    adapter_down_weight,
    adapter_up_weight,
):
    rows, width = tokens.shape
    owned, rank, features = adapter_up_weight.shape
    adapters = adapter_position.shape[0]
    chips = replicas // 2
    parts = CHUNKS + 1
    ids = jnp.arange(adapters, dtype=jnp.int32)[:, None, None]
    named = token_adapter.reshape(1, rows // LANES, LANES) == ids
    slots = jnp.sum(jnp.where(named, adapter_position[:, None, None], 0), axis=0)
    any_space = pl.BlockSpec(memory_space=pl.ANY)
    vmem = pl.BlockSpec(memory_space=pltpu.VMEM)
    dma = pltpu.SemaphoreType.DMA
    values, _, _ = pl.pallas_call(
        functools.partial(gather_kernel, replicas, rank),
        out_shape=(
            jax.ShapeDtypeStruct((rows, features), jnp.bfloat16),
            jax.ShapeDtypeStruct((adapters, rank, width), jnp.bfloat16),
            jax.ShapeDtypeStruct((adapters, rank, features), jnp.bfloat16),
        ),
        in_specs=[any_space] * 4 + [vmem],
        out_specs=(vmem, any_space, any_space),
        scratch_shapes=[
            pltpu.VMEM((rows, width), jnp.bfloat16),
            pltpu.VMEM((2, BASE_DEPTH, features), jnp.bfloat16),
            pltpu.VMEM((4 * rank, width // CHUNKS), jnp.bfloat16),
            pltpu.VMEM((4 * rank, features), jnp.bfloat16),
            pltpu.VMEM((rows, 1), jnp.int32),
            pltpu.VMEM((rows, features), jnp.float32),
            pltpu.VMEM((rows, 4 * rank), jnp.float32),
            dma((CHUNKS,)),
            dma((2,)),
            dma((4, 2)),
            dma(((chips - 1) * 2 * parts,)),
            dma(((chips - 1) * 2 * parts,)),
            dma((chips * 2 * parts,)),
            dma((chips * 2 * parts,)),
        ],
        compiler_params=pltpu.CompilerParams(
            collective_id=0, has_side_effects=True, vmem_limit_bytes=52 * 2**20
        ),
        cost_estimate=pl.CostEstimate(
            flops=2 * rows * width * (features + adapters * rank)
            + 2 * rows * features * adapters * rank,
            bytes_accessed=2 * (rows * width + width * features + 3 * adapters * rank * width),
            transcendentals=0,
        ),
        name="gather_and_project",
    )(
        tokens,
        value_weight,
        adapter_down_weight,
        adapter_up_weight,
        slots,
    )
    alive = jnp.arange(rows, dtype=jnp.int32) < replica_live_rows[0]
    return jnp.where(alive[:, None], values, jnp.zeros_like(values))


def split_shards(
    tokens,
    token_adapter,
    adapter_position,
    replica_live_rows,
    value_weight,
    adapter_down_weight,
    adapter_up_weight,
):
    rows = tokens.shape[0]
    adapters = adapter_position.shape[0]
    rank = adapter_up_weight.shape[1]
    every_down = lax.all_gather(adapter_down_weight, "replica", axis=0, tiled=True)
    every_up = lax.all_gather(adapter_up_weight, "replica", axis=0, tiled=True)
    base = lax.psum_scatter(
        jnp.dot(tokens, value_weight, preferred_element_type=jnp.float32),
        "tensor",
        scatter_dimension=1,
        tiled=True,
    )
    ids = jnp.arange(adapters, dtype=jnp.int32)[None, :]
    slot = jnp.sum(jnp.where(token_adapter == ids, adapter_position[None, :], 0), axis=1)
    hot = slot[:, None] == ids
    partial = jnp.einsum("td,ard->tar", tokens, every_down, preferred_element_type=jnp.float32)
    partial = jnp.sum(jnp.where(hot[:, :, None], partial, 0.0), axis=1)
    shrunk = lax.psum(partial, "tensor").astype(jnp.bfloat16)
    spread = jnp.where(hot[:, :, None], shrunk[:, None, :], jnp.zeros((), jnp.bfloat16))
    delta = jnp.dot(
        spread.reshape(rows, adapters * rank),
        every_up.reshape(adapters * rank, -1),
        preferred_element_type=jnp.float32,
    ).astype(jnp.bfloat16)
    alive = jnp.arange(rows, dtype=jnp.int32) < replica_live_rows[0]
    return jnp.where(alive[:, None], base + delta.astype(jnp.float32), 0.0).astype(jnp.bfloat16)


def solution(mesh):
    in_specs = (
        P(("group", "replica"), "tensor"),
        P(("group", "replica"), None),
        P("group"),
        P(("group", "replica")),
        P("tensor", None),
        P(("group", "replica"), None, "tensor"),
        P(("group", "replica"), None, "tensor"),
    )
    out_specs = P(("group", "replica"), "tensor")
    if mesh.shape["tensor"] == 1:
        body = functools.partial(ring_shards, mesh.shape["replica"])
    else:
        body = split_shards
    return jax.shard_map(body, mesh=mesh, in_specs=in_specs, out_specs=out_specs, check_vma=False)
```
